32 devices in a mesh: prow: 8 (over z, x), pcol: 4 (over y, core).
Axes of the slice: x: 2, y: 2, z: 4, core: 2. Of those that a mesh axis runs over, the one named last changes fastest.
Arguments:
- matrix: bfloat16 [16384, 4096], P('prow', 'pcol'), may hold values from -6 to 6
- inverses: bfloat16 [2, 512, 512], replicated, may hold values from -0.01171875 to 0.01171875
Outputs:
- factored: bfloat16 [16384, 4096], P('prow', 'pcol')
The draws below stay inside these ranges and needn't reach their ends.
All inputs are finite; a program needn't handle non-finite values.
Results may differ from the reference program's by a relative error of at most 0.0063.
Values may be sent and summed in bfloat16 or wider, within the bound.
A program may use at most 64 MiB of HBM per device.

```python
import jax
import jax.numpy as jnp
from jax import lax

NB = 512
STEPS = 2
ROWS_DEV = 2048
COLS_DEV = 1024
N_ROWS = 16384
N_COLS = 4096
N_PROW = 8
N_PCOL = 4


def steps_of(rng, shape, shards, least, high):
    def one(dim, parts):
        heights = jax.random.uniform(jax.random.fold_in(jax.random.fold_in(rng, 6), dim), (parts,), jnp.float32, least / len(shards), high / len(shards))
        return jnp.repeat(jnp.exp(heights), shape[dim] // parts).reshape((-1,) + (1,) * (len(shape) - dim - 1))

    gain = one(*shards[0])
    for cut in shards[1:]:
        gain = gain * one(*cut)
    return gain


def normal_values(own_key, dims, deviation, limit, split=(), kind=jnp.bfloat16):
    drawn = jax.random.normal(own_key, dims, jnp.float32) * deviation
    if len(split) > 0:
        drawn = steps_of(own_key, dims, split, -0.22, 0.18) * drawn
    return jnp.clip(drawn, min=-limit, max=limit).astype(kind)


def setup_inputs(seed: int = 0) -> dict:
    key_of = jax.random.split(jax.random.key(seed), 3)
    return {
        "matrix": normal_values(key_of[0], (N_ROWS, N_COLS), 1.0, 6.0, ((0, 8), (1, 4))),
        "inverses": normal_values(key_of[1], (STEPS, NB, NB), (NB * NB) ** -0.5, 0.01171875),
    }


def stored_start(logical, held, count):
    per = held // NB
    return ((logical % count) * per + logical // count) * NB


def advance(current, step_index, upper, inverses, col_logical):
    start = stored_start(step_index, COLS_DEV, N_PCOL)
    panel = current[:, start:start + NB].astype(jnp.bfloat16)
    lower = jnp.dot(panel, inverses[step_index], preferred_element_type=jnp.float32).astype(jnp.bfloat16)
    update = jnp.dot(lower, upper, preferred_element_type=jnp.float32)
    right = (col_logical > step_index)[None, :]
    current = current - jnp.where(right, update, jnp.float32(0.0))
    return current.at[:, start:start + NB].set(lower.astype(jnp.float32))


def reference(matrix, inverses):
    col_stored = jnp.arange(N_COLS, dtype=jnp.int32) // NB
    col_per = COLS_DEV // NB
    col_logical = (col_stored % col_per) * N_PCOL + col_stored // col_per
    uppers = []
    for block in range(STEPS):
        start = stored_start(block, ROWS_DEV, N_PROW)
        current = matrix[start:start + NB].astype(jnp.float32)
        for step_index in range(block):
            current = advance(current, step_index, uppers[step_index], inverses, col_logical)
        uppers.append(current.astype(jnp.bfloat16))
    row_per = ROWS_DEV // NB
    blocks = matrix.reshape(N_ROWS // NB, NB, N_COLS)
    stored_index = jnp.arange(N_ROWS // NB, dtype=jnp.int32)
    row_logical = (stored_index % row_per) * N_PROW + stored_index // row_per

    def one_block(item):
        rows_in, logical = item
        current = rows_in.astype(jnp.float32)
        for step_index in range(STEPS):
            moved = advance(current, step_index, uppers[step_index], inverses, col_logical)
            current = jnp.where(logical > step_index, moved, current)
        return current.astype(jnp.bfloat16)

    result = lax.map(one_block, (blocks, row_logical))
    return result.reshape(N_ROWS, N_COLS)
```

```python
import functools

import jax
import jax.numpy as jnp
from jax import lax
from jax.experimental import pallas as pl
from jax.experimental.pallas import tpu as pltpu
from jax.sharding import PartitionSpec as P

MESH = pl.DeviceIdType.MESH
ROW_CHUNK = 256
COL_CHUNK = 128
U01_PARTS = 2


def kernel(
    n_rows, n_cols, m, inv, out,
    cur, res, pan, low, u, u01, ivm,
    load_sem, inv_sem, out_sem,
    y_send, y_recv, s_send, s_recv,
    z_send, z_recv, x_send, x_recv,
    c_send, cz_send, cx_send, cs_send, c_recv,
):
    p = lax.axis_index("prow")
    q = lax.axis_index("pcol")
    chip, core = q // 2, q % 2
    chips = n_cols // 2
    par = p % 2
    block = inv.shape[1]
    rows_dev, cols_dev = m.shape
    ny = rows_dev // ROW_CHUNK
    nb = block // ROW_CHUNK
    nu = cols_dev // COL_CHUNK
    part = block // U01_PARTS
    sib = q + 1 - 2 * core
    mate = p + 1 - 2 * par
    origin = jnp.logical_and(p == 0, q == 1)

    def rows_of(j):
        return pl.ds(pl.multiple_of(j * ROW_CHUNK, ROW_CHUNK), ROW_CHUNK)

    def cols_of(n):
        return pl.ds(pl.multiple_of(n * COL_CHUNK, COL_CHUNK), COL_CHUNK)

    def part_of(i):
        return pl.ds(i * part, part)

    def need(k, j):
        return jnp.logical_or(j * ROW_CHUNK >= block, p > k)

    def when(*conds):
        return pl.when(functools.reduce(jnp.logical_and, conds))

    def wait(ref, sem):
        pltpu.make_async_copy(ref, ref, sem).wait()

    def send(ref, send_sem, recv_sem, to):
        pltpu.make_async_remote_copy(
            src_ref=ref, dst_ref=ref, send_sem=send_sem, recv_sem=recv_sem,
            device_id=to, device_id_type=MESH,
        ).start()

    def u_ref(h, n):
        return u.at[pl.ds(pl.multiple_of(h * block, block), block), cols_of(n)]

    @when(p == 0)
    def _():
        @pl.loop(0, nu)
        def _(n):
            pltpu.make_async_copy(
                m.at[pl.ds(0, block), cols_of(n)], u_ref(0, n), z_recv.at[n]
            ).start()

    @when(origin)
    def _():
        for i in range(U01_PARTS):
            pltpu.make_async_copy(
                m.at[pl.ds(0, block), part_of(i)], u01.at[:, part_of(i)], c_recv.at[i]
            ).start()

    @when(chip == 0)
    def _():
        @pl.loop(0, ny)
        def _(j):
            @when(need(core, j))
            def _():
                pltpu.make_async_copy(
                    m.at[rows_of(j), pl.ds(0, block)], pan.at[core, rows_of(j)], y_recv.at[j]
                ).start()

    pltpu.make_async_copy(inv, ivm, inv_sem).start()
    pltpu.make_async_copy(m, cur, load_sem).start()

    barrier = pltpu.get_barrier_semaphore()

    def greet(to):
        pl.semaphore_signal(barrier, inc=1, device_id=to, device_id_type=MESH)

    greet((p, sib))
    greet((mate, q))
    up, down = chip + 1 < chips, chip > 0
    ahead, behind = p + 2 < n_rows, p >= 2

    @when(up)
    def _():
        greet((p, q + 2))

    @when(down)
    def _():
        greet((p, q - 2))

    @when(ahead)
    def _():
        greet((p + 2, q))

    @when(behind)
    def _():
        greet((p - 2, q))

    count = 2
    for cond in (up, down, ahead, behind):
        count = count + cond.astype(jnp.int32)
    pl.semaphore_wait(barrier, count)

    def panel_step(j):
        @when(need(core, j))
        def _():
            mine = pan.at[core, rows_of(j)]
            wait(mine, y_recv.at[j])

            @when(up)
            def _():
                send(mine, y_send.at[j], y_recv.at[j], (p, q + 2))

            send(mine, s_send.at[j], s_recv.at[j], (p, sib))

    def lower0(j):
        rows = rows_of(j)

        @when(need(0, j), core == 1)
        def _():
            wait(pan.at[0, rows], s_recv.at[j])

        @when(need(0, j))
        def _():
            low[rows, :block] = jnp.dot(
                pan[0, rows, :], ivm[0], preferred_element_type=jnp.float32
            ).astype(low.dtype)

        @when(jnp.logical_not(need(0, j)))
        def _():
            low[rows, :block] = jnp.zeros((ROW_CHUNK, block), low.dtype)

    def lower1(j):
        rows = rows_of(j)

        @when(need(1, j), core == 0)
        def _():
            wait(pan.at[1, rows], s_recv.at[j])

        @when(need(1, j))
        def _():
            panel = (
                pan[1, rows, :].astype(jnp.float32)
                - jnp.dot(low[rows, :block], u01[...], preferred_element_type=jnp.float32)
            ).astype(low.dtype)
            low[rows, block:] = jnp.dot(
                panel, ivm[1], preferred_element_type=jnp.float32
            ).astype(low.dtype)

        @when(jnp.logical_not(need(1, j)))
        def _():
            low[rows, block:] = jnp.zeros((ROW_CHUNK, block), low.dtype)

    def update(j):
        rows = rows_of(j)

        def plain(b):
            cols = slice(b * block, (b + 1) * block)
            res[rows, cols] = (
                cur[rows, cols].astype(jnp.float32)
                - jnp.dot(low[rows, :], u[:, cols], preferred_element_type=jnp.float32)
            ).astype(res.dtype)

        for k in range(2):
            @when(q == k, need(k, j))
            def _(k=k):
                res[rows, :block] = low[rows, k * block : (k + 1) * block]

        @when(jnp.logical_not(jnp.logical_and(chip == 0, need(core, j))))
        def _():
            plain(0)

        for b in range(1, cols_dev // block):
            plain(b)
        pltpu.make_async_copy(res.at[rows], out.at[rows], out_sem.at[j]).start()

    def u_step(n):
        @when(p == 1)
        def _():
            wait(u_ref(0, n), x_recv.at[n])
            cols = cols_of(n)
            u[block:, cols] = (
                cur[:block, cols].astype(jnp.float32)
                - jnp.dot(low[:block, :block], u[:block, cols], preferred_element_type=jnp.float32)
            ).astype(u.dtype)

        @when(p != 1)
        def _():
            wait(u_ref(par, n), z_recv.at[n])

        @when(ahead)
        def _():
            send(u_ref(par, n), z_send.at[n], z_recv.at[n], (p + 2, q))

        send(u_ref(par, n), x_send.at[n], x_recv.at[n], (mate, q))

    def u01_right(i):
        @when(p == 0, up)
        def _():
            send(u01.at[:, part_of(i)], c_send.at[i], c_recv.at[i], (p, q + 2))

    @when(origin)
    def _():
        for i in range(U01_PARTS):
            wait(u01.at[:, part_of(i)], c_recv.at[i])
            u01_right(i)

    @when(p == 0)
    def _():
        @pl.loop(0, nu)
        def _(n):
            u_step(n)

    @when(jnp.logical_or(chip == 0, p == 1))
    def _():
        @pl.loop(0, nb)
        def _(j):
            panel_step(j)

    wait(ivm, inv_sem)
    wait(cur, load_sem)

    early = 2

    @when(p == 1)
    def _():
        @pl.loop(0, nb)
        def _(j):
            lower0(j)

        @pl.loop(0, early)
        def _(n):
            u_step(n)

    @when(chip == 0)
    def _():
        @pl.loop(nb, ny)
        def _(j):
            panel_step(j)

    def later_panel(j):
        @when(chip > 0, jnp.logical_or(p != 1, j >= nb))
        def _():
            panel_step(j)

    @when(p > 0)
    def _():
        @pl.loop(jnp.where(p == 1, early, 0), nu)
        def _(n):
            u_step(n)

    @when(core == 1)
    def _():
        for i in range(U01_PARTS):
            mine = u01.at[:, part_of(i)]

            @when(jnp.logical_not(origin))
            def _():
                wait(mine, c_recv.at[i])
                u01_right(i)

            send(mine, cs_send.at[i], c_recv.at[i], (p, sib))

            @when(par == 0)
            def _():
                @when(ahead)
                def _():
                    send(mine, cz_send.at[i], c_recv.at[i], (p + 2, q))

                send(mine, cx_send.at[i], c_recv.at[i], (mate, q))

    @when(core == 0)
    def _():
        for i in range(U01_PARTS):
            wait(u01.at[:, part_of(i)], c_recv.at[i])

    @when(p != 1)
    def _():
        @pl.loop(0, nu)
        def _(n):
            wait(u_ref(1 - par, n), x_recv.at[n])

    @pl.loop(0, ny)
    def _(j):
        later_panel(j)

        @when(jnp.logical_or(p != 1, j >= nb))
        def _():
            lower0(j)

        lower1(j)
        update(j)

    @pl.loop(0, ny)
    def _(j):
        wait(res.at[rows_of(j)], out_sem.at[j])

        @when(need(core, j))
        def _():
            mine = pan.at[core, rows_of(j)]
            wait(mine, s_send.at[j])

            @when(up)
            def _():
                wait(mine, y_send.at[j])

    @pl.loop(0, nu)
    def _(n):
        wait(u_ref(par, n), x_send.at[n])

        @when(ahead)
        def _():
            wait(u_ref(par, n), z_send.at[n])

    @when(core == 1)
    def _():
        for i in range(U01_PARTS):
            mine = u01.at[:, part_of(i)]
            wait(mine, cs_send.at[i])

            @when(p == 0, up)
            def _():
                wait(mine, c_send.at[i])

            @when(par == 0)
            def _():
                wait(mine, cx_send.at[i])

                @when(ahead)
                def _():
                    wait(mine, cz_send.at[i])


def per_device(n_rows, n_cols, matrix, inverses):
    rows_dev, cols_dev = matrix.shape
    block = inverses.shape[1]
    kind = matrix.dtype
    ny, nu = rows_dev // ROW_CHUNK, cols_dev // COL_CHUNK
    dma = pltpu.SemaphoreType.DMA
    return pl.pallas_call(
        functools.partial(kernel, n_rows, n_cols),
        out_shape=jax.ShapeDtypeStruct(matrix.shape, kind),
        in_specs=[pl.BlockSpec(memory_space=pl.ANY)] * 2,
        out_specs=pl.BlockSpec(memory_space=pl.ANY),
        scratch_shapes=[
            pltpu.VMEM((rows_dev, cols_dev), kind),
            pltpu.VMEM((rows_dev, cols_dev), kind),
            pltpu.VMEM((2, rows_dev, block), kind),
            pltpu.VMEM((rows_dev, 2 * block), kind),
            pltpu.VMEM((2 * block, cols_dev), kind),
            pltpu.VMEM((block, block), kind),
            pltpu.VMEM(inverses.shape, kind),
            dma, dma, dma((ny,)),
            dma((ny,)), dma((ny,)), dma((ny,)), dma((ny,)),
            dma((nu,)), dma((nu,)), dma((nu,)), dma((nu,)),
            dma((U01_PARTS,)), dma((U01_PARTS,)), dma((U01_PARTS,)), dma((U01_PARTS,)),
            dma((U01_PARTS,)),
        ],
        compiler_params=pltpu.CompilerParams(
            collective_id=0, has_side_effects=True, vmem_limit_bytes=44 * 2**20
        ),
    )(matrix, inverses)


def solution(mesh):
    body = functools.partial(per_device, mesh.shape["prow"], mesh.shape["pcol"])
    return jax.shard_map(
        body, mesh=mesh, in_specs=(P("prow", "pcol"), P()),
        out_specs=P("prow", "pcol"), check_vma=False,
    )
```

```python
import functools

import jax
import jax.numpy as jnp
from jax import lax
from jax.experimental import pallas as pl
from jax.experimental.pallas import tpu as pltpu
from jax.sharding import PartitionSpec as P

MESH = pl.DeviceIdType.MESH
ROW_CHUNK = 512
SEND_ROWS = 128
WINDOW = 6
HELD_BACK = 2
U01_AT = 8
COL_CHUNK = 128
U01_PARTS = 2


def kernel(
    n_rows, n_cols, m, inv, out,
    cur, res, pan, low, u, u01, ivm,
    load_sem, inv_sem, out_sem,
    y_send, y_recv, s_send, s_recv,
    z_send, z_recv, x_send, x_recv,
    c_send, cz_send, cx_send, cs_send, c_recv,
):
    p = lax.axis_index("prow")
    q = lax.axis_index("pcol")
    chip, core = q // 2, q % 2
    chips = n_cols // 2
    par = p % 2
    block = inv.shape[1]
    rows_dev, cols_dev = m.shape
    ny = rows_dev // SEND_ROWS
    nb = block // SEND_ROWS
    nr = rows_dev // ROW_CHUNK
    per = ROW_CHUNK // SEND_ROWS
    nu = cols_dev // COL_CHUNK
    part = block // U01_PARTS
    sib = q + 1 - 2 * core
    mate = p + 1 - 2 * par
    origin = jnp.logical_and(p == 0, q == 1)

    def rows_of(j):
        return pl.ds(pl.multiple_of(j * ROW_CHUNK, ROW_CHUNK), ROW_CHUNK)

    def sent_rows(j):
        return pl.ds(pl.multiple_of(j * SEND_ROWS, SEND_ROWS), SEND_ROWS)

    def cols_of(n):
        return pl.ds(pl.multiple_of(n * COL_CHUNK, COL_CHUNK), COL_CHUNK)

    def part_of(i):
        return pl.ds(i * part, part)

    def need(k, j):
        return jnp.logical_or(j * ROW_CHUNK >= block, p > k)

    def sent(k, j):
        return jnp.logical_or(j * SEND_ROWS >= block, p > k)

    def when(*conds):
        return pl.when(functools.reduce(jnp.logical_and, conds))

    def wait(ref, sem):
        pltpu.make_async_copy(ref, ref, sem).wait()

    def send(ref, send_sem, recv_sem, to):
        pltpu.make_async_remote_copy(
            src_ref=ref, dst_ref=ref, send_sem=send_sem, recv_sem=recv_sem,
            device_id=to, device_id_type=MESH,
        ).start()

    def u_ref(h, n):
        return u.at[pl.ds(pl.multiple_of(h * block, block), block), cols_of(n)]

    @when(p == 0)
    def _():
        @pl.loop(0, nu)
        def _(n):
            pltpu.make_async_copy(
                m.at[pl.ds(0, block), cols_of(n)], u_ref(0, n), z_recv.at[n]
            ).start()

    @when(origin)
    def _():
        for i in range(U01_PARTS):
            pltpu.make_async_copy(
                m.at[pl.ds(0, block), part_of(i)], u01.at[:, part_of(i)], c_recv.at[i]
            ).start()

    @when(chip == 0)
    def _():
        @pl.loop(0, ny)
        def _(j):
            @when(sent(core, j))
            def _():
                pltpu.make_async_copy(
                    m.at[sent_rows(j), pl.ds(0, block)], pan.at[core, sent_rows(j)], y_recv.at[j]
                ).start()

    pltpu.make_async_copy(inv, ivm, inv_sem).start()
    pltpu.make_async_copy(m, cur, load_sem).start()

    barrier = pltpu.get_barrier_semaphore()

    def greet(to):
        pl.semaphore_signal(barrier, inc=1, device_id=to, device_id_type=MESH)

    greet((p, sib))
    greet((mate, q))
    up, down = chip + 1 < chips, chip > 0
    ahead, behind = p + 2 < n_rows, p >= 2

    @when(up)
    def _():
        greet((p, q + 2))

    @when(down)
    def _():
        greet((p, q - 2))

    @when(ahead)
    def _():
        greet((p + 2, q))

    @when(behind)
    def _():
        greet((p - 2, q))

    count = 2
    for cond in (up, down, ahead, behind):
        count = count + cond.astype(jnp.int32)
    pl.semaphore_wait(barrier, count)

    def panel_step(j):
        @when(up, j >= WINDOW, sent(core, j - WINDOW))
        def _():
            wait(pan.at[core, sent_rows(j - WINDOW)], y_send.at[j - WINDOW])

        @when(sent(core, j))
        def _():
            mine = pan.at[core, sent_rows(j)]
            wait(mine, y_recv.at[j])

            @when(up)
            def _():
                send(mine, y_send.at[j], y_recv.at[j], (p, q + 2))

            send(mine, s_send.at[j], s_recv.at[j], (p, sib))

    def lower0(j):
        rows = rows_of(j)

        @when(need(0, j), core == 1)
        def _():
            for i in range(per):
                wait(pan.at[0, sent_rows(j * per + i)], s_recv.at[j * per + i])

        @when(need(0, j))
        def _():
            low[rows, :block] = jnp.dot(
                pan[0, rows, :], ivm[0], preferred_element_type=jnp.float32
            ).astype(low.dtype)

        @when(jnp.logical_not(need(0, j)))
        def _():
            low[rows, :block] = jnp.zeros((ROW_CHUNK, block), low.dtype)

    def lower1(j):
        rows = rows_of(j)

        @when(need(1, j), core == 0)
        def _():
            for i in range(per):
                wait(pan.at[1, sent_rows(j * per + i)], s_recv.at[j * per + i])

        @when(need(1, j))
        def _():
            panel = (
                pan[1, rows, :].astype(jnp.float32)
                - jnp.dot(low[rows, :block], u01[...], preferred_element_type=jnp.float32)
            ).astype(low.dtype)
            low[rows, block:] = jnp.dot(
                panel, ivm[1], preferred_element_type=jnp.float32
            ).astype(low.dtype)

        @when(jnp.logical_not(need(1, j)))
        def _():
            low[rows, block:] = jnp.zeros((ROW_CHUNK, block), low.dtype)

    def update(j):
        rows = rows_of(j)

        def plain(first, last):
            cols = slice(first, last)
            res[rows, cols] = (
                cur[rows, cols].astype(jnp.float32)
                - jnp.dot(low[rows, :], u[:, cols], preferred_element_type=jnp.float32)
            ).astype(res.dtype)

        for k in range(2):
            @when(q == k, need(k, j))
            def _(k=k):
                res[rows, :block] = low[rows, k * block : (k + 1) * block]

        special = jnp.logical_and(chip == 0, need(core, j))

        @when(jnp.logical_not(special))
        def _():
            plain(0, cols_dev)

        @when(special)
        def _():
            plain(block, cols_dev)

        pltpu.make_async_copy(res.at[rows], out.at[rows], out_sem.at[j]).start()

    def u_step(n):
        @when(p == 1)
        def _():
            wait(u_ref(0, n), x_recv.at[n])
            cols = cols_of(n)
            u[block:, cols] = (
                cur[:block, cols].astype(jnp.float32)
                - jnp.dot(low[:block, :block], u[:block, cols], preferred_element_type=jnp.float32)
            ).astype(u.dtype)

        @when(p != 1)
        def _():
            wait(u_ref(par, n), z_recv.at[n])

        @when(ahead)
        def _():
            send(u_ref(par, n), z_send.at[n], z_recv.at[n], (p + 2, q))

        send(u_ref(par, n), x_send.at[n], x_recv.at[n], (mate, q))

    def u01_right(i):
        @when(p == 0, up)
        def _():
            send(u01.at[:, part_of(i)], c_send.at[i], c_recv.at[i], (p, q + 2))

    def u01_step(i):
        mine = u01.at[:, part_of(i)]

        @when(jnp.logical_not(origin))
        def _():
            wait(mine, c_recv.at[i])

        @when(core == 1)
        def _():
            @when(jnp.logical_not(origin))
            def _():
                u01_right(i)

            send(mine, cs_send.at[i], c_recv.at[i], (p, sib))

            @when(par == 0)
            def _():
                @when(ahead)
                def _():
                    send(mine, cz_send.at[i], c_recv.at[i], (p + 2, q))

                send(mine, cx_send.at[i], c_recv.at[i], (mate, q))

    def prow_step(n):
        for i in range(U01_PARTS):
            @when(n == U01_AT + i)
            def _(i=i):
                u01_step(i)

        @when(n < U01_AT)
        def _():
            u_step(n)

        @when(n >= U01_AT + U01_PARTS)
        def _():
            u_step(n - U01_PARTS)

    prow_steps = nu + U01_PARTS

    @when(origin)
    def _():
        for i in range(U01_PARTS):
            wait(u01.at[:, part_of(i)], c_recv.at[i])
            u01_right(i)

    ahead_of = 2

    @when(p == 0)
    def _():
        @pl.loop(0, ahead_of)
        def _(n):
            prow_step(n)

    wait(ivm, inv_sem)

    @when(p == 1)
    def _():
        @pl.loop(0, nb)
        def _(j):
            panel_step(j)

        @pl.loop(0, nb // per)
        def _(j):
            lower0(j)

        wait(cur, load_sem)

        @pl.loop(0, ahead_of)
        def _(n):
            prow_step(n)

    @when(p != 1)
    def _():
        wait(cur, load_sem)

    hops = p // 2 + par
    lag = jnp.where(chip == 0, WINDOW, 0)
    offset = jnp.where(p == 0, ahead_of, 1 - hops - lag)
    slots = jnp.where(chip == 0, ny, ny - HELD_BACK)

    @pl.loop(0, slots)
    def _(t):
        @when(jnp.logical_or(p != 1, t >= nb))
        def _():
            panel_step(t)

        n = t + offset

        @when(n >= jnp.where(p <= 1, ahead_of, 0), n < prow_steps)
        def _():
            prow_step(n)

        j = t // per - 1

        @when(t % per == per - 1, j >= jnp.where(p == 1, nb // per, 0))
        def _():
            lower0(j)

    @pl.loop(jnp.clip(slots + offset, 0, prow_steps), prow_steps)
    def _(n):
        prow_step(n)

    @when(p != 1)
    def _():
        @pl.loop(0, nu)
        def _(n):
            wait(u_ref(1 - par, n), x_recv.at[n])

    lowered = slots // per - 1

    @pl.loop(0, nr)
    def _(j):
        t = slots + j - (nr - 1 - HELD_BACK)

        @when(t >= slots, t < ny)
        def _():
            panel_step(t)

        @when(j >= lowered)
        def _():
            lower0(j)

        lower1(j)
        update(j)

    @pl.loop(0, nr)
    def _(j):
        wait(res.at[rows_of(j)], out_sem.at[j])

    @pl.loop(0, ny)
    def _(j):
        @when(sent(core, j))
        def _():
            mine = pan.at[core, sent_rows(j)]
            wait(mine, s_send.at[j])

            @when(up, j >= ny - WINDOW)
            def _():
                wait(mine, y_send.at[j])

    @pl.loop(0, nu)
    def _(n):
        wait(u_ref(par, n), x_send.at[n])

        @when(ahead)
        def _():
            wait(u_ref(par, n), z_send.at[n])

    @when(core == 1)
    def _():
        for i in range(U01_PARTS):
            mine = u01.at[:, part_of(i)]
            wait(mine, cs_send.at[i])

            @when(p == 0, up)
            def _():
                wait(mine, c_send.at[i])

            @when(par == 0)
            def _():
                wait(mine, cx_send.at[i])

                @when(ahead)
                def _():
                    wait(mine, cz_send.at[i])


def per_device(n_rows, n_cols, matrix, inverses):
    rows_dev, cols_dev = matrix.shape
    block = inverses.shape[1]
    kind = matrix.dtype
    ny, nu, nr = rows_dev // SEND_ROWS, cols_dev // COL_CHUNK, rows_dev // ROW_CHUNK
    dma = pltpu.SemaphoreType.DMA
    return pl.pallas_call(
        functools.partial(kernel, n_rows, n_cols),
        out_shape=jax.ShapeDtypeStruct(matrix.shape, kind),
        in_specs=[pl.BlockSpec(memory_space=pl.ANY)] * 2,
        out_specs=pl.BlockSpec(memory_space=pl.ANY),
        scratch_shapes=[
            pltpu.VMEM((rows_dev, cols_dev), kind),
            pltpu.VMEM((rows_dev, cols_dev), kind),
            pltpu.VMEM((2, rows_dev, block), kind),
            pltpu.VMEM((rows_dev, 2 * block), kind),
            pltpu.VMEM((2 * block, cols_dev), kind),
            pltpu.VMEM((block, block), kind),
            pltpu.VMEM(inverses.shape, kind),
            dma, dma, dma((nr,)),
            dma((ny,)), dma((ny,)), dma((ny,)), dma((ny,)),
            dma((nu,)), dma((nu,)), dma((nu,)), dma((nu,)),
            dma((U01_PARTS,)), dma((U01_PARTS,)), dma((U01_PARTS,)), dma((U01_PARTS,)),
            dma((U01_PARTS,)),
        ],
        compiler_params=pltpu.CompilerParams(
            collective_id=0, has_side_effects=True, vmem_limit_bytes=60 * 2**20
        ),
    )(matrix, inverses)


def solution(mesh):
    body = functools.partial(per_device, mesh.shape["prow"], mesh.shape["pcol"])
    return jax.shard_map(
        body, mesh=mesh, in_specs=(P("prow", "pcol"), P()),
        out_specs=P("prow", "pcol"), check_vma=False,
    )
```

```python
import functools

import jax
import jax.numpy as jnp
from jax import lax
from jax.experimental import pallas as pl
from jax.experimental.pallas import tpu as pltpu
from jax.sharding import PartitionSpec as P

MESH = pl.DeviceIdType.MESH
ROW_CHUNK = 512
SEND_ROWS = 64
WINDOW = 12
HELD_BACK = 4
U01_AT = 16
COL_CHUNK = 128
U01_PARTS = 4
U_HALVES = 2


def kernel(
    n_rows, n_cols, m, inv, out,
    cur, res, pan, low, u, u01, ivm,
    load_sem, inv_sem, out_sem,
    y_send, y_recv, s_send, s_recv,
    z_send, z_recv, x_send, x_recv,
    c_send, cz_send, cx_send, cs_send, c_recv,
):
    p = lax.axis_index("prow")
    q = lax.axis_index("pcol")
    chip, core = q // 2, q % 2
    chips = n_cols // 2
    par = p % 2
    block = inv.shape[1]
    rows_dev, cols_dev = m.shape
    ny = rows_dev // SEND_ROWS
    nb = block // SEND_ROWS
    nr = rows_dev // ROW_CHUNK
    per = ROW_CHUNK // SEND_ROWS
    nu = U_HALVES * (cols_dev // COL_CHUNK)
    half = block // U_HALVES
    part = block // U01_PARTS
    sib = q + 1 - 2 * core
    mate = p + 1 - 2 * par
    origin = jnp.logical_and(p == 0, q == 1)

    def rows_of(j):
        return pl.ds(pl.multiple_of(j * ROW_CHUNK, ROW_CHUNK), ROW_CHUNK)

    def sent_rows(j):
        return pl.ds(pl.multiple_of(j * SEND_ROWS, SEND_ROWS), SEND_ROWS)

    def cols_of(n):
        return pl.ds(pl.multiple_of(n * COL_CHUNK, COL_CHUNK), COL_CHUNK)

    def part_of(i):
        return pl.ds(i * part, part)

    def need(k, j):
        return jnp.logical_or(j * ROW_CHUNK >= block, p > k)

    def sent(k, j):
        return jnp.logical_or(j * SEND_ROWS >= block, p > k)

    def when(*conds):
        return pl.when(functools.reduce(jnp.logical_and, conds))

    def wait(ref, sem):
        pltpu.make_async_copy(ref, ref, sem).wait()

    def send(ref, send_sem, recv_sem, to):
        pltpu.make_async_remote_copy(
            src_ref=ref, dst_ref=ref, send_sem=send_sem, recv_sem=recv_sem,
            device_id=to, device_id_type=MESH,
        ).start()

    def u_ref(h, n):
        first = h * block + n % U_HALVES * half
        return u.at[pl.ds(pl.multiple_of(first, half), half), cols_of(n // U_HALVES)]

    @when(p == 0)
    def _():
        @pl.loop(0, nu)
        def _(n):
            pltpu.make_async_copy(
                m.at[
                    pl.ds(pl.multiple_of(n % U_HALVES * half, half), half),
                    cols_of(n // U_HALVES),
                ],
                u_ref(0, n),
                z_recv.at[n],
            ).start()

    @when(origin)
    def _():
        for i in range(U01_PARTS):
            pltpu.make_async_copy(
                m.at[pl.ds(0, block), part_of(i)], u01.at[:, part_of(i)], c_recv.at[i]
            ).start()

    @when(chip == 0)
    def _():
        @pl.loop(0, ny)
        def _(j):
            @when(sent(core, j))
            def _():
                pltpu.make_async_copy(
                    m.at[sent_rows(j), pl.ds(0, block)], pan.at[core, sent_rows(j)], y_recv.at[j]
                ).start()

    pltpu.make_async_copy(inv, ivm, inv_sem).start()
    pltpu.make_async_copy(m, cur, load_sem).start()

    barrier = pltpu.get_barrier_semaphore()

    def greet(to):
        pl.semaphore_signal(barrier, inc=1, device_id=to, device_id_type=MESH)

    greet((p, sib))
    greet((mate, q))
    up, down = chip + 1 < chips, chip > 0
    ahead, behind = p + 2 < n_rows, p >= 2

    @when(up)
    def _():
        greet((p, q + 2))

    @when(down)
    def _():
        greet((p, q - 2))

    @when(ahead)
    def _():
        greet((p + 2, q))

    @when(behind)
    def _():
        greet((p - 2, q))

    count = 2
    for cond in (up, down, ahead, behind):
        count = count + cond.astype(jnp.int32)
    pl.semaphore_wait(barrier, count)

    def panel_step(j):
        @when(up, j >= WINDOW, sent(core, j - WINDOW))
        def _():
            wait(pan.at[core, sent_rows(j - WINDOW)], y_send.at[j - WINDOW])

        @when(sent(core, j))
        def _():
            mine = pan.at[core, sent_rows(j)]
            wait(mine, y_recv.at[j])

            @when(up)
            def _():
                send(mine, y_send.at[j], y_recv.at[j], (p, q + 2))

            send(mine, s_send.at[j], s_recv.at[j], (p, sib))

    def lower0(j):
        rows = rows_of(j)

        @when(need(0, j), core == 1)
        def _():
            for i in range(per):
                wait(pan.at[0, sent_rows(j * per + i)], s_recv.at[j * per + i])

        @when(need(0, j))
        def _():
            low[rows, :block] = jnp.dot(
                pan[0, rows, :], ivm[0], preferred_element_type=jnp.float32
            ).astype(low.dtype)

        @when(jnp.logical_not(need(0, j)))
        def _():
            low[rows, :block] = jnp.zeros((ROW_CHUNK, block), low.dtype)

    def lower1(j):
        rows = rows_of(j)

        @when(need(1, j), core == 0)
        def _():
            for i in range(per):
                wait(pan.at[1, sent_rows(j * per + i)], s_recv.at[j * per + i])

        @when(need(1, j))
        def _():
            panel = (
                pan[1, rows, :].astype(jnp.float32)
                - jnp.dot(low[rows, :block], u01[...], preferred_element_type=jnp.float32)
            ).astype(low.dtype)
            low[rows, block:] = jnp.dot(
                panel, ivm[1], preferred_element_type=jnp.float32
            ).astype(low.dtype)

        @when(jnp.logical_not(need(1, j)))
        def _():
            low[rows, block:] = jnp.zeros((ROW_CHUNK, block), low.dtype)

    def update(j):
        rows = rows_of(j)

        def plain(first, last):
            cols = slice(first, last)
            res[rows, cols] = (
                cur[rows, cols].astype(jnp.float32)
                - jnp.dot(low[rows, :], u[:, cols], preferred_element_type=jnp.float32)
            ).astype(res.dtype)

        for k in range(2):
            @when(q == k, need(k, j))
            def _(k=k):
                res[rows, :block] = low[rows, k * block : (k + 1) * block]

        special = jnp.logical_and(chip == 0, need(core, j))

        @when(jnp.logical_not(special))
        def _():
            plain(0, cols_dev)

        @when(special)
        def _():
            plain(block, cols_dev)

        pltpu.make_async_copy(res.at[rows], out.at[rows], out_sem.at[j]).start()

    def u_step(n):
        @when(p == 1, n % U_HALVES == 0)
        def _():
            for i in range(U_HALVES):
                wait(u_ref(0, n + i), x_recv.at[n + i])
            cols = cols_of(n // U_HALVES)
            u[block:, cols] = (
                cur[:block, cols].astype(jnp.float32)
                - jnp.dot(low[:block, :block], u[:block, cols], preferred_element_type=jnp.float32)
            ).astype(u.dtype)

        @when(p != 1)
        def _():
            wait(u_ref(par, n), z_recv.at[n])

        @when(ahead)
        def _():
            send(u_ref(par, n), z_send.at[n], z_recv.at[n], (p + 2, q))

        send(u_ref(par, n), x_send.at[n], x_recv.at[n], (mate, q))

    def u01_right(i):
        @when(p == 0, up)
        def _():
            send(u01.at[:, part_of(i)], c_send.at[i], c_recv.at[i], (p, q + 2))

    def u01_step(i):
        mine = u01.at[:, part_of(i)]

        @when(jnp.logical_not(origin))
        def _():
            wait(mine, c_recv.at[i])

        @when(core == 1)
        def _():
            @when(jnp.logical_not(origin))
            def _():
                u01_right(i)

            send(mine, cs_send.at[i], c_recv.at[i], (p, sib))

            @when(par == 0)
            def _():
                @when(ahead)
                def _():
                    send(mine, cz_send.at[i], c_recv.at[i], (p + 2, q))

                send(mine, cx_send.at[i], c_recv.at[i], (mate, q))

    def prow_step(n):
        for i in range(U01_PARTS):
            @when(n == U01_AT + i)
            def _(i=i):
                u01_step(i)

        @when(n < U01_AT)
        def _():
            u_step(n)

        @when(n >= U01_AT + U01_PARTS)
        def _():
            u_step(n - U01_PARTS)

    prow_steps = nu + U01_PARTS

    @when(origin)
    def _():
        for i in range(U01_PARTS):
            wait(u01.at[:, part_of(i)], c_recv.at[i])
            u01_right(i)

    ahead_of = 4

    @when(p == 0)
    def _():
        @pl.loop(0, ahead_of)
        def _(n):
            prow_step(n)

    wait(ivm, inv_sem)

    @when(p == 1)
    def _():
        @pl.loop(0, nb)
        def _(j):
            panel_step(j)

        @pl.loop(0, nb // per)
        def _(j):
            lower0(j)

        wait(cur, load_sem)

        @pl.loop(0, ahead_of)
        def _(n):
            prow_step(n)

    @when(p != 1)
    def _():
        wait(cur, load_sem)

    hops = p // 2 + par
    lag = jnp.where(chip == 0, WINDOW, 0)
    offset = jnp.where(p == 0, ahead_of, 1 - 2 * hops - lag)
    slots = jnp.where(chip == 0, ny, jnp.minimum(ny - HELD_BACK, prow_steps + 2 * hops))

    @pl.loop(0, slots)
    def _(t):
        @when(jnp.logical_or(p != 1, t >= nb))
        def _():
            panel_step(t)

        n = t + offset

        @when(n >= jnp.where(p <= 1, ahead_of, 0), n < prow_steps)
        def _():
            prow_step(n)

        j = t // per - 1

        @when(t % per == per - 1, j >= jnp.where(p == 1, nb // per, 0))
        def _():
            lower0(j)

    @pl.loop(jnp.clip(slots + offset, 0, prow_steps), prow_steps)
    def _(n):
        prow_step(n)

    @when(p != 1)
    def _():
        @pl.loop(0, nu)
        def _(n):
            wait(u_ref(1 - par, n), x_recv.at[n])

    lowered = slots // per - 1

    @pl.loop(0, nr)
    def _(j):
        @pl.loop(jnp.maximum(slots, per * j), jnp.maximum(slots, per * (j + 1)))
        def _(t):
            panel_step(t)

        @when(j >= lowered)
        def _():
            lower0(j)

        lower1(j)
        update(j)

    @pl.loop(0, nr)
    def _(j):
        wait(res.at[rows_of(j)], out_sem.at[j])

    @pl.loop(0, ny)
    def _(j):
        @when(sent(core, j))
        def _():
            mine = pan.at[core, sent_rows(j)]
            wait(mine, s_send.at[j])

            @when(up, j >= ny - WINDOW)
            def _():
                wait(mine, y_send.at[j])

    @pl.loop(0, nu)
    def _(n):
        wait(u_ref(par, n), x_send.at[n])

        @when(ahead)
        def _():
            wait(u_ref(par, n), z_send.at[n])

    @when(core == 1)
    def _():
        for i in range(U01_PARTS):
            mine = u01.at[:, part_of(i)]
            wait(mine, cs_send.at[i])

            @when(p == 0, up)
            def _():
                wait(mine, c_send.at[i])

            @when(par == 0)
            def _():
                wait(mine, cx_send.at[i])

                @when(ahead)
                def _():
                    wait(mine, cz_send.at[i])


def per_device(n_rows, n_cols, matrix, inverses):
    rows_dev, cols_dev = matrix.shape
    block = inverses.shape[1]
    kind = matrix.dtype
    ny, nu, nr = rows_dev // SEND_ROWS, U_HALVES * (cols_dev // COL_CHUNK), rows_dev // ROW_CHUNK
    dma = pltpu.SemaphoreType.DMA
    return pl.pallas_call(
        functools.partial(kernel, n_rows, n_cols),
        out_shape=jax.ShapeDtypeStruct(matrix.shape, kind),
        in_specs=[pl.BlockSpec(memory_space=pl.ANY)] * 2,
        out_specs=pl.BlockSpec(memory_space=pl.ANY),
        scratch_shapes=[
            pltpu.VMEM((rows_dev, cols_dev), kind),
            pltpu.VMEM((rows_dev, cols_dev), kind),
            pltpu.VMEM((2, rows_dev, block), kind),
            pltpu.VMEM((rows_dev, 2 * block), kind),
            pltpu.VMEM((2 * block, cols_dev), kind),
            pltpu.VMEM((block, block), kind),
            pltpu.VMEM(inverses.shape, kind),
            dma, dma, dma((nr,)),
            dma((ny,)), dma((ny,)), dma((ny,)), dma((ny,)),
            dma((nu,)), dma((nu,)), dma((nu,)), dma((nu,)),
            dma((U01_PARTS,)), dma((U01_PARTS,)), dma((U01_PARTS,)), dma((U01_PARTS,)),
            dma((U01_PARTS,)),
        ],
        compiler_params=pltpu.CompilerParams(
            collective_id=0, has_side_effects=True, vmem_limit_bytes=60 * 2**20
        ),
    )(matrix, inverses)


def solution(mesh):
    body = functools.partial(per_device, mesh.shape["prow"], mesh.shape["pcol"])
    return jax.shard_map(
        body, mesh=mesh, in_specs=(P("prow", "pcol"), P()),
        out_specs=P("prow", "pcol"), check_vma=False,
    )
```
